32 devices in a mesh: dp: 8 (over y, x, core), ctx: 4 (over z).
Axes of the slice: x: 2, y: 2, z: 4, core: 2. Of those that a mesh axis runs over, the one named last changes fastest.
Arguments:
- layer_input: bfloat16 [8, 640, 8192], P('dp', 'ctx'), may hold values from -6 to 6
- query_rows: bfloat16 [8, 640, 1024], P('dp', 'ctx'), may hold values from -8 to 8
- key_rows: bfloat16 [8, 640, 128], P('dp', 'ctx'), may hold values from -8 to 8
- value_rows: bfloat16 [8, 640, 128], P('dp', 'ctx'), may hold values from -6 to 6
- grad_out: bfloat16 [8, 640, 1024], P('dp', 'ctx'), may hold values from -6 to 6
- doc_lengths: int32 [8, 8], P('dp'), may hold values from 1 to 320, 640 in all within a row
- block_order: int32 [8], replicated, may hold values from 0 to 7, each once
Outputs:
- query_grad: bfloat16 [8, 640, 1024], P('dp', 'ctx')
- weight_grad: bfloat16 [8192, 256], P(('dp', 'ctx'))
The draws below stay inside these ranges and needn't reach their ends.
Inputs may be any that keep to these rules, and one draw needn't show every extreme that they name: `block_order`: each number of 0 to 7 appears once. `doc_lengths`: the lengths of a row sum to 640; the longest of each row is half of 640.
All inputs are finite; a program needn't handle non-finite values.
Results may differ from the reference program's by a relative error of at most 0.01.
Values may be sent and summed in bfloat16 or wider, within the bound.
A program may use at most 64 MiB of HBM per device.

```python
import math
import jax
import jax.numpy as jnp
import numpy as np
from jax import lax

D = 8192
HEADS = 8
HEAD_DIM = 128
DOCS = 8
TOK_DEV = 160
SEQ = 640
BLOCK = 80
NBLK = 8
BATCH = 8


def draw_key_rows(key, part):
    shape = (BATCH, SEQ, HEAD_DIM)
    drawn_key = jax.random.fold_in(key, 1)
    return jnp.clip(jax.random.normal(drawn_key, shape, jnp.float32), -6.0, 6.0).astype(jnp.bfloat16)


def draw_query_rows(key, part):
    shape = (BATCH, SEQ, HEADS * HEAD_DIM)
    drawn_key = jax.random.fold_in(key, 2)
    return jnp.clip(jax.random.normal(drawn_key, shape, jnp.float32), -6.0, 6.0).astype(jnp.bfloat16)


def raised(drawn, stream_key, source, target, parts, factor):
    def block_of(dim):
        return (jnp.arange(drawn.shape[dim]) // (drawn.shape[dim] // parts)).reshape((-1,) + (1,) * (drawn.ndim - 1 - dim))

    one_side = jax.random.permutation(stream_key, parts)[block_of(target)]
    other_side = (block_of(target) + parts // 2) % parts
    return jnp.where((block_of(source) == one_side) | (block_of(source) == other_side), factor * drawn, drawn)


def shard_levels(own_key, shape, cuts, smallest, largest):
    gain, own = 1.0, jax.random.fold_in(own_key, 6)
    for dim, blocks in cuts:
        heights = jnp.exp(jax.random.uniform(jax.random.fold_in(own, dim), (blocks,), jnp.float32, smallest / len(cuts), largest / len(cuts)))
        gain = gain * jnp.repeat(heights, shape[dim] // blocks).reshape([-1 if axis == dim else 1 for axis in range(len(shape))])
    return gain


def split_up(count, total, reach, slope):
    portions = [(1 << 20) // math.isqrt(rank ** slope) + 1 for rank in range(2, count + 1)]
    spare, holding = total - reach - (count - 1), [1] * (count - 1)
    while spare > 0:
        candidates = [i for i in range(count - 1) if holding[i] < reach]
        mass, left = sum([portions[i] for i in candidates]), spare
        for i in candidates:
            extra = min(reach - holding[i], max(1, left * portions[i] // mass), spare)
            holding[i] = holding[i] + extra
            spare = spare - extra
    return np.array([reach] + holding)


def ragged(own_key, count, total, most, skew):
    if count == 2:
        one = jax.random.randint(own_key, (), max(1, total - most), min(most, total - 1) + 1)
        return jnp.stack([one, total - one])
    tallies = jnp.asarray(split_up(count, total, most, skew), jnp.int32)
    twos = (count - 1) // 2
    donor, sink = tallies[1:1 + 2 * twos:2], tallies[2:2 + 2 * twos:2]
    room = jnp.minimum(donor - 1, most - sink)
    moved = jax.random.randint(jax.random.fold_in(own_key, 1), (twos,), 0, 1 << 20) % (room + 1)
    tallies = tallies.at[1:1 + 2 * twos:2].set(donor - moved).at[2:2 + 2 * twos:2].set(sink + moved)
    return tallies[jax.random.permutation(jax.random.fold_in(own_key, 2), count)]


def noise(own_key, extent, width, bound, cuts=(), kind=jnp.bfloat16):
    level = shard_levels(own_key, extent, cuts, -0.22, 0.18) if cuts else 1.0
    entries = jax.random.normal(own_key, extent, jnp.float32) * width * level
    return jnp.minimum(jnp.maximum(entries, -bound), bound).astype(kind)


def bell_draw_with(key, extent, width, reach, cuts, heavy, held_as=jnp.bfloat16):
    drawn = width * jax.random.normal(key, extent, jnp.float32)
    if cuts:
        drawn = drawn * shard_levels(key, extent, cuts, -0.22, 0.18)
    return jnp.clip(raised(drawn, jax.random.fold_in(key, 3), *heavy), -reach, reach).astype(held_as)


def setup_inputs(seed: int = 0) -> dict:
    key_of = jax.random.split(jax.random.key(seed), 8)
    return {
        "layer_input": bell_draw_with(key_of[0], (BATCH, SEQ, D), 1.0, 6.0, ((0, 8), (1, 4)), (1, 2, 4, 2.0)),
        "query_rows": draw_query_rows(jax.random.fold_in(key_of[7], 71), 0),
        "key_rows": draw_key_rows(jax.random.fold_in(key_of[7], 71), 0),
        "value_rows": noise(key_of[3], (BATCH, SEQ, HEAD_DIM), 1.0, 6.0, ((0, 8), (1, 4))),
        "grad_out": noise(key_of[4], (BATCH, SEQ, HEADS * HEAD_DIM), 1.0, 6.0, ((0, 8), (1, 4))),
        "doc_lengths": jax.vmap(lambda own: ragged(own, DOCS, SEQ, SEQ // 2, 2))(jax.random.split(key_of[5], BATCH)).reshape((BATCH, DOCS)).astype(jnp.int32),
        "block_order": jax.random.permutation(key_of[6], NBLK).astype(jnp.int32),
    }


def token_positions(block_order):
    rows = jnp.arange(SEQ, dtype=jnp.int32)
    blocks = jnp.take(block_order, rows // BLOCK)
    return (blocks * BLOCK + rows % BLOCK).astype(jnp.int32)


def document_ids(position, lengths):
    ends = jnp.cumsum(lengths).astype(jnp.int32)
    return jnp.sum((ends[None, :] <= position[:, None]).astype(jnp.int32), axis=1).astype(jnp.int32)


def reference(layer_input, query_rows, key_rows, value_rows, grad_out, doc_lengths, block_order):
    scale = HEAD_DIM ** -0.5
    position = token_positions(block_order)

    def one_row(summed, items):
        inputs, queries, keyset, valueset, grads, lengths = items
        document = document_ids(position, lengths)

        def one_block(accum, start):
            qblock = lax.dynamic_slice_in_dim(queries, start, TOK_DEV, 0).reshape(TOK_DEV * HEADS, HEAD_DIM)
            gblock = lax.dynamic_slice_in_dim(grads, start, TOK_DEV, 0).reshape(TOK_DEV * HEADS, HEAD_DIM)
            qpos = lax.dynamic_slice_in_dim(position, start, TOK_DEV, 0)
            qdoc = lax.dynamic_slice_in_dim(document, start, TOK_DEV, 0)
            allowed = (qdoc[:, None] == document[None, :]) & (position[None, :] <= qpos[:, None])
            allowed = jnp.repeat(allowed, HEADS, axis=0)
            scores = jnp.dot(qblock, keyset.T, preferred_element_type=jnp.float32) * scale
            masked = jnp.where(allowed, scores, -jnp.inf)
            best = jnp.max(masked, axis=1, keepdims=True)
            total = jnp.sum(jnp.where(allowed, jnp.exp(masked - best), 0.0), axis=1, keepdims=True)
            lse = best + jnp.log(total)
            probs = jnp.where(allowed, jnp.exp(masked - lse), 0.0)
            dprobs = jnp.dot(gblock, valueset.T, preferred_element_type=jnp.float32)
            delta = jnp.sum(probs * dprobs, axis=1, keepdims=True)
            dscores = (probs * (dprobs - delta)).astype(jnp.bfloat16)
            weights = probs.astype(jnp.bfloat16)
            dquery = (jnp.dot(dscores, keyset, preferred_element_type=jnp.float32) * scale).astype(jnp.bfloat16)
            dkey = jnp.dot(dscores.T, qblock, preferred_element_type=jnp.float32)
            dvalue = jnp.dot(weights.T, gblock, preferred_element_type=jnp.float32)
            return accum + jnp.concatenate([dkey, dvalue], axis=1), dquery.reshape(TOK_DEV, HEADS * HEAD_DIM)

        starts = jnp.arange(SEQ // TOK_DEV, dtype=jnp.int32) * TOK_DEV
        pair_sum, dquery = lax.scan(one_block, jnp.zeros((SEQ, 2 * HEAD_DIM), jnp.float32), starts)
        column = jnp.where(jnp.arange(2 * HEAD_DIM) < HEAD_DIM, scale, 1.0)
        pair_grad = (pair_sum * column[None, :]).astype(jnp.bfloat16)
        summed = summed + jnp.dot(inputs.T, pair_grad, preferred_element_type=jnp.float32)
        return summed, dquery.reshape(SEQ, HEADS * HEAD_DIM)

    summed, query_grad = lax.scan(one_row, jnp.zeros((D, 2 * HEAD_DIM), jnp.float32),
                                  (layer_input, query_rows, key_rows, value_rows, grad_out, doc_lengths))
    weight_grad = (summed * (BATCH * SEQ) ** -0.5).astype(jnp.bfloat16)
    return query_grad, weight_grad
```

```python
import math

import jax
import jax.numpy as jnp
from jax import lax
from jax.experimental import pallas as pl
from jax.experimental.pallas import tpu as pltpu
from jax.sharding import PartitionSpec as P


def passed_along(value, axis, steps):
    count = lax.axis_size(axis)
    pairs = [(source, (source + steps) % count) for source in range(count)]
    return lax.ppermute(value, axis, pairs)


def shard_positions(block_order, owner, rows):
    half = rows // 2
    local = jnp.arange(rows, dtype=jnp.int32)
    first = lax.dynamic_index_in_dim(block_order, 2 * owner, 0, keepdims=False)
    second = lax.dynamic_index_in_dim(block_order, 2 * owner + 1, 0, keepdims=False)
    blocks = jnp.where(local < half, first, second)
    return blocks * half + local % half


def document_ids(position, ends):
    return jnp.sum((ends[None, :] <= position[:, None]).astype(jnp.int32), axis=1)


def document_ends(lengths):
    index = jnp.arange(lengths.shape[0])
    return jnp.sum(jnp.where(index[None, :] <= index[:, None], lengths[None, :], 0), axis=1)


def contract_rows(left, right):
    return lax.dot_general(
        left, right, (((0,), (0,)), ((), ())), preferred_element_type=jnp.float32
    )


def contract_cols(left, right):
    return lax.dot_general(
        left, right, (((1,), (1,)), ((), ())), preferred_element_type=jnp.float32
    )


def by_rings(layer_input, query_rows, key_rows, value_rows, grad_out, doc_lengths, block_order):
    rows = query_rows.shape[1]
    width = key_rows.shape[2]
    heads = query_rows.shape[2] // width
    parts = lax.axis_size("ctx")
    me = lax.axis_index("ctx")
    scale = width ** (-0.5)
    ends = document_ends(doc_lengths[0])
    queries = query_rows[0].reshape(rows * heads, width)
    grads = grad_out[0].reshape(rows * heads, width)
    own_pos = shard_positions(block_order, me, rows)
    query_pos = jnp.repeat(own_pos, heads)
    query_doc = jnp.repeat(document_ids(own_pos, ends), heads)
    paired = jnp.concatenate([key_rows[0], value_rows[0]], axis=1)
    query_zero = jnp.zeros((rows * heads, width), jnp.float32)
    pair_zero = jnp.zeros((rows, 2 * width), jnp.float32)

    def allowed_for(owner):
        key_pos = shard_positions(block_order, owner, rows)
        key_doc = document_ids(key_pos, ends)
        return (query_doc[:, None] == key_doc[None, :]) & (key_pos[None, :] <= query_pos[:, None])

    def forward_terms(state, block, allowed):
        best, total, weighted = state
        scores = contract_cols(queries, block[:, :width]) * scale
        masked = jnp.where(allowed, scores, -jnp.inf)
        new_best = jnp.maximum(best, jnp.max(masked, axis=1))
        safe_best = jnp.where(jnp.isfinite(new_best), new_best, 0.0)
        probs = jnp.where(allowed, jnp.exp(masked - safe_best[:, None]), 0.0)
        dprobs = contract_cols(grads, block[:, width:])
        factor = jnp.exp(best - safe_best)
        return (
            new_best,
            total * factor + jnp.sum(probs, axis=1),
            weighted * factor + jnp.sum(probs * dprobs, axis=1),
        )

    def forward_step(state, block, owner):
        allowed = allowed_for(owner)
        return forward_terms(state, block, allowed)

    def backward_terms(block, allowed, lse, delta):
        scores = contract_cols(queries, block[:, :width]) * scale
        probs = jnp.where(allowed, jnp.exp(scores - lse[:, None]), 0.0)
        dprobs = contract_cols(grads, block[:, width:])
        dscores = (probs * (dprobs - delta[:, None])).astype(jnp.bfloat16)
        weights = probs.astype(jnp.bfloat16)
        dquery = jnp.dot(dscores, block[:, :width], preferred_element_type=jnp.float32)
        dpair = jnp.concatenate(
            [contract_rows(dscores, queries), contract_rows(weights, grads)], axis=1
        )
        return (dquery, dpair)

    def backward_step(block, owner, lse, delta):
        allowed = allowed_for(owner)
        return backward_terms(block, allowed, lse, delta)

    start_state = (
        jnp.full((rows * heads,), -jnp.inf, jnp.float32),
        jnp.zeros((rows * heads,), jnp.float32),
        jnp.zeros((rows * heads,), jnp.float32),
    )

    def forward_turn(turn, carry):
        state, block = carry
        state = forward_step(state, block, (me - turn) % parts)
        block = passed_along(block, "ctx", 1)
        return (state, block)

    state, block = lax.fori_loop(0, parts - 1, forward_turn, (start_state, paired))
    best, total, weighted = forward_step(state, block, (me + 1) % parts)
    lse = best + jnp.log(total)
    delta = weighted / total

    def backward_turn(turn, carry):
        block, pair_grad, dquery = carry
        add_query, add_pair = backward_step(block, (me - turn) % parts, lse, delta)
        pair_grad = passed_along((pair_grad + add_pair).astype(jnp.bfloat16), "ctx", 1).astype(
            jnp.float32
        )
        block = passed_along(block, "ctx", 1)
        return (block, pair_grad, dquery + add_query)

    block, pair_grad, dquery = lax.fori_loop(
        0, parts, backward_turn, (paired, pair_zero, query_zero)
    )
    column = jnp.where(jnp.arange(2 * width) < width, scale, 1.0)
    pair_low = (pair_grad * column[None, :]).astype(jnp.bfloat16)
    inputs = layer_input[0]
    summed = lax.psum_scatter(
        contract_rows(inputs, pair_low), ("dp", "ctx"), scatter_dimension=0, tiled=True
    )
    grad_scale = (lax.axis_size("dp") * rows * parts) ** (-0.5)
    weight_grad = (summed * grad_scale).astype(jnp.bfloat16)
    query_grad = (dquery * scale).astype(jnp.bfloat16).reshape(1, rows, heads * width)
    return (query_grad, weight_grad)


def kernel(
    grad_scale, x_ref, q_ref, k_ref, v_ref, g_ref, len_ref, order_ref, dq_ref, dw_ref,
    qs, gs, kbuf, vbuf, probs, dprobs, dscores, part, landed, pair, xa, xb,
    early, cross, crossed, zsum, zout, zland,
    k_send, k_recv, v_send, v_recv, x_send, x_recv, own_sem, part_send, part_recv,
    pair_send, pair_recv, cross_send, cross_recv, z_send, z_recv,
):
    rows, width = k_ref.shape
    heads = q_ref.shape[1] // width
    half = rows // 2
    lanes = rows * heads
    chunk = dw_ref.shape[0]
    parts = 4
    dp, me = lax.axis_index("dp"), lax.axis_index("ctx")
    y, x, c = dp // 4, (dp // 2) % 2, dp % 2

    def place(yy, xx, cc):
        return (yy * 2 + xx) * 2 + cc

    def remote(source, target, send, recv, where):
        return pltpu.make_async_remote_copy(
            src_ref=source, dst_ref=target, send_sem=send, recv_sem=recv,
            device_id=where, device_id_type=pl.DeviceIdType.MESH,
        )

    peers = [(dp, (me + s) % parts) for s in range(1, parts)]
    near = [
        (y, x, 1 - c), (y, 1 - x, c), (y, 1 - x, 1 - c), (1 - y, x, c), (1 - y, x, 1 - c),
    ]
    close = [(place(*n), me) for n in near]

    barrier = pltpu.get_barrier_semaphore()
    for where in peers + close:
        pl.semaphore_signal(barrier, inc=1, device_id=where, device_id_type=pl.DeviceIdType.MESH)

    for h in range(heads):
        qs[h * rows:(h + 1) * rows, :] = q_ref[:, h * width:(h + 1) * width]
        gs[h * rows:(h + 1) * rows, :] = g_ref[:, h * width:(h + 1) * width]
    kbuf[0] = k_ref[...]
    vbuf[0] = v_ref[...]

    pl.semaphore_wait(barrier, len(peers) + len(close))

    sent, kcopies, vcopies = [], [None], [None]
    for s in range(1, parts):
        where = peers[s - 1]
        kcopies.append(remote(k_ref, kbuf.at[s], k_send.at[s], k_recv.at[s], where))
        vcopies.append(remote(v_ref, vbuf.at[s], v_send.at[s], v_recv.at[s], where))
    for s in (2, 1, 3):
        kcopies[s].start()
    for s in (2, 1, 3):
        vcopies[s].start()
    sent += kcopies[1:] + vcopies[1:]

    xcopies, owned = [], []
    for slot, (cx, cc) in enumerate([(x, c), (x, 1 - c), (1 - x, c), (1 - x, 1 - c)]):
        for t in range(2):
            first = pl.multiple_of(place(t, cx, cc) * (parts * chunk), parts * chunk)
            source = x_ref.at[:, pl.ds(first, 2 * chunk)]
            target = xa.at[t, pl.ds(slot * rows, rows), :]
            if slot == 0:
                owned.append(pltpu.make_async_copy(source, target, own_sem.at[t]))
            else:
                n = slot * 2 + t
                xcopies.append(remote(source, target, x_send.at[0, n], x_recv.at[0, n], (place(y, cx, cc), me)))
    for slot, (cy, cc) in enumerate([(y, c), (y, 1 - c), (1 - y, c), (1 - y, 1 - c)]):
        for t in range(2):
            first = pl.multiple_of(place(cy, t, cc) * (parts * chunk) + 2 * chunk, 2 * chunk)
            source = x_ref.at[:, pl.ds(first, 2 * chunk)]
            target = xb.at[t, pl.ds(slot * rows, rows), :]
            if slot == 0:
                owned.append(pltpu.make_async_copy(source, target, own_sem.at[2 + t]))
            else:
                n = slot * 2 + t
                xcopies.append(remote(source, target, x_send.at[1, n], x_recv.at[1, n], (place(cy, x, cc), me)))
    for copy in xcopies + owned:
        copy.start()
    sent += xcopies

    lane = lax.broadcasted_iota(jnp.int32, (1, lanes), 1)
    inside = lane
    for h in range(1, heads):
        inside = inside - jnp.where(lane >= h * rows, rows, 0)
    first = (order_ref[2 * me]) * half
    second = (order_ref[2 * me + 1] - 1) * half
    qpos = inside + jnp.where(inside < half, first, second)
    begin = jnp.zeros((1, lanes), jnp.int32)
    end = jnp.int32(0)
    for j in range(len_ref.shape[1]):
        end = end + len_ref[0, j]
        begin = jnp.where(qpos >= end, end, begin)
    row = lax.broadcasted_iota(jnp.int32, (rows, 1), 0)

    def nt(left, right):
        return lax.dot_general(left, right, (((1,), (1,)), ((), ())), preferred_element_type=jnp.float32)

    def nn(left, right):
        return jnp.dot(left, right, preferred_element_type=jnp.float32)

    scale = width ** (-0.5)
    base2 = scale * math.log2(math.e)
    order = (0, 1, 3, 2)
    best = None
    for s in order:
        if s:
            kcopies[s].wait_recv()
        owner = (me - s + parts) % parts
        one = (order_ref[2 * owner]) * half
        two = (order_ref[2 * owner + 1] - 1) * half
        kpos = row + jnp.where(row < half, one, two)
        allowed = (kpos >= begin) & (kpos <= qpos)
        scores = jnp.where(allowed, nt(kbuf[s], qs[...]) * base2, -1e30)
        probs[s] = scores
        top = jnp.max(scores, axis=0, keepdims=True)
        best = top if best is None else jnp.maximum(best, top)
    total, weighted = 0.0, 0.0
    for s in order:
        if s:
            vcopies[s].wait_recv()
        prob = jnp.exp2(probs[s] - best)
        dprob = nt(vbuf[s], gs[...])
        probs[s] = prob
        dprobs[s] = dprob
        total = total + jnp.sum(prob, axis=0, keepdims=True)
        weighted = weighted + jnp.sum(prob * dprob, axis=0, keepdims=True)
    inverse = 1.0 / total
    delta = weighted * inverse

    partcopies = [None]
    for s in range(1, parts):
        where = (dp, (me - s + parts) % parts)
        partcopies.append(remote(part.at[s], landed.at[s], part_send.at[s], part_recv.at[s], where))
    own_pair = None
    for s in (2, 1, 3, 0):
        prob = probs[s] * inverse
        dscore = (prob * (dprobs[s] - delta)).astype(jnp.bfloat16)
        dscores[s * rows:(s + 1) * rows, :] = dscore
        dkey = nn(dscore, qs[...])
        dvalue = nn(prob.astype(jnp.bfloat16), gs[...])
        if s:
            part[s, :, :width] = dkey.astype(jnp.bfloat16)
            part[s, :, width:] = dvalue.astype(jnp.bfloat16)
            partcopies[s].start()
        else:
            own_pair = (dkey, dvalue)
    sent += partcopies[1:]

    keys = kbuf[...].reshape(parts * rows, width)
    dquery = nn(keys.T, dscores[...]) * scale
    for h in range(heads):
        dq_ref[:, h * width:(h + 1) * width] = (
            dquery[:, h * rows:(h + 1) * rows].T.astype(jnp.bfloat16)
        )

    dkey, dvalue = own_pair
    for s in (1, 3, 2):
        partcopies[s].wait_recv()
        dkey = dkey + landed[s, :, :width].astype(jnp.float32)
        dvalue = dvalue + landed[s, :, width:].astype(jnp.float32)
    pair[0:rows, :width] = (dkey * scale).astype(jnp.bfloat16)
    pair[0:rows, width:] = dvalue.astype(jnp.bfloat16)
    paircopies = [None]
    for n in range(1, 6):
        copy = remote(
            pair.at[pl.ds(0, rows), :], pair.at[pl.ds(n * rows, rows), :],
            pair_send.at[n], pair_recv.at[n], close[n - 1],
        )
        paircopies.append(copy)
    for n in (3, 5, 2, 4, 1):
        paircopies[n].start()
    sent += paircopies[1:]

    for copy in owned:
        copy.wait()
    for copy in xcopies:
        copy.wait_recv()
    paircopies[1].wait_recv()
    turned = pair[0:2 * rows, :].T
    for t in range(2):
        early[0, t] = nn(turned, xa[t, 0:2 * rows, :])
        early[1, t] = nn(turned, xb[t, 0:2 * rows, :])
    crosscopies = [[], []]
    kept = (y, x)
    away = [(place(1 - y, x, c), me), (place(y, 1 - x, c), me)]
    for a in range(2):
        for z in range(2):
            crosscopies[a].append(remote(
                cross.at[a, z], crossed.at[a, z], cross_send.at[a, z], cross_recv.at[a, z], away[a],
            ))
    turns = []
    for a, xs in enumerate((xa, xb)):
        paircopies[2 + 2 * a].wait_recv()
        paircopies[3 + 2 * a].wait_recv()
        turned = pair[(2 + 2 * a) * rows:(4 + 2 * a) * rows, :].T
        turns.append(turned)
        other = 1 - kept[a]
        for z in range(2):
            cols = slice(z * chunk, (z + 1) * chunk)
            made = early[a, other, :, cols] + nn(turned, xs[other, 2 * rows:4 * rows, cols])
            cross[a, z] = made.astype(jnp.bfloat16)
            crosscopies[a][z].start()
    for a, xs in enumerate((xa, xb)):
        for z in range(2):
            cols = slice(z * chunk, (z + 1) * chunk)
            zsum[2 * a + z] = early[a, kept[a], :, cols] + nn(turns[a], xs[kept[a], 2 * rows:4 * rows, cols])
        sent += crosscopies[a]

    for z, a in ((0, 0), (1, 0), (0, 1), (1, 1)):
        t = 2 * a + z
        crosscopies[a][z].wait_recv()
        made = zsum[t] + crossed[a, z].astype(jnp.float32)
        zsum[t] = made
        zout[t] = made.astype(jnp.bfloat16)

        @pl.when(me != t)
        def _():
            s = (t - me + parts) % parts
            remote(zout.at[t], zland.at[s], z_send.at[s], z_recv.at[s], (dp, t)).start()

    final = zsum[me]
    for s in (1, 3, 2):
        to = (me + s) % parts
        copy = remote(zout.at[to], zland.at[s], z_send.at[s], z_recv.at[s], (dp, to))
        copy.wait_recv()
        final = final + zland[s].astype(jnp.float32)
        sent.append(copy)
    dw_ref[...] = (final * grad_scale).T.astype(jnp.bfloat16)
    for copy in sent:
        copy.wait_send()


def fused(layer_input, query_rows, key_rows, value_rows, grad_out, doc_lengths, block_order):
    rows, width = key_rows.shape[1:]
    model = layer_input.shape[2]
    heads = query_rows.shape[2] // width
    count, parts = lax.axis_size("dp"), lax.axis_size("ctx")
    chunk = model // (count * parts)
    lanes = rows * heads
    grad_scale = (count * rows * parts) ** (-0.5)
    low, full = jnp.bfloat16, jnp.float32
    vmem = pl.BlockSpec(memory_space=pltpu.VMEM)
    smem = pl.BlockSpec(memory_space=pltpu.SMEM)
    dma = pltpu.SemaphoreType.DMA

    def body(*refs):
        kernel(grad_scale, *refs)

    query_grad, weight_grad = pl.pallas_call(
        body,
        out_shape=(
            jax.ShapeDtypeStruct((rows, heads * width), low),
            jax.ShapeDtypeStruct((chunk, 2 * width), low),
        ),
        in_specs=[pl.BlockSpec(memory_space=pl.ANY), vmem, vmem, vmem, vmem, smem, smem],
        out_specs=(vmem, vmem),
        scratch_shapes=[
            pltpu.VMEM((lanes, width), low),
            pltpu.VMEM((lanes, width), low),
            pltpu.VMEM((parts, rows, width), low),
            pltpu.VMEM((parts, rows, width), low),
            pltpu.VMEM((parts, rows, lanes), full),
            pltpu.VMEM((parts, rows, lanes), full),
            pltpu.VMEM((parts * rows, lanes), low),
            pltpu.VMEM((parts, rows, 2 * width), low),
            pltpu.VMEM((parts, rows, 2 * width), low),
            pltpu.VMEM((6 * rows, 2 * width), low),
            pltpu.VMEM((2, 4 * rows, 2 * chunk), low),
            pltpu.VMEM((2, 4 * rows, 2 * chunk), low),
            pltpu.VMEM((2, 2, 2 * width, 2 * chunk), full),
            pltpu.VMEM((2, 2, 2 * width, chunk), low),
            pltpu.VMEM((2, 2, 2 * width, chunk), low),
            pltpu.VMEM((4, 2 * width, chunk), full),
            pltpu.VMEM((4, 2 * width, chunk), low),
            pltpu.VMEM((4, 2 * width, chunk), low),
            dma((4,)), dma((4,)), dma((4,)), dma((4,)),
            dma((2, 8)), dma((2, 8)), dma((4,)),
            dma((4,)), dma((4,)), dma((6,)), dma((6,)),
            dma((2, 2)), dma((2, 2)), dma((4,)), dma((4,)),
        ],
        compiler_params=pltpu.CompilerParams(
            collective_id=0, has_side_effects=True, vmem_limit_bytes=48 * 1024 * 1024
        ),
    )(layer_input[0], query_rows[0], key_rows[0], value_rows[0], grad_out[0], doc_lengths, block_order)
    return (query_grad[None], weight_grad)


def solution(mesh):
    placed = (
        P("dp", "ctx", None),
        P("dp", "ctx", None),
        P("dp", "ctx", None),
        P("dp", "ctx", None),
        P("dp", "ctx", None),
        P("dp", None),
        P(),
    )
    return jax.shard_map(
        fused if dict(mesh.shape) == {"dp": 8, "ctx": 4} else by_rings,
        mesh=mesh,
        in_specs=placed,
        out_specs=(P("dp", "ctx", None), P(("dp", "ctx"), None)),
        check_vma=False,
    )
```

```python
import math

import jax
import jax.numpy as jnp
from jax import lax
from jax.experimental import pallas as pl
from jax.experimental.pallas import tpu as pltpu
from jax.sharding import PartitionSpec as P


def passed_along(value, axis, steps):
    count = lax.axis_size(axis)
    pairs = [(source, (source + steps) % count) for source in range(count)]
    return lax.ppermute(value, axis, pairs)


def shard_positions(block_order, owner, rows):
    half = rows // 2
    local = jnp.arange(rows, dtype=jnp.int32)
    first = lax.dynamic_index_in_dim(block_order, 2 * owner, 0, keepdims=False)
    second = lax.dynamic_index_in_dim(block_order, 2 * owner + 1, 0, keepdims=False)
    blocks = jnp.where(local < half, first, second)
    return blocks * half + local % half


def document_ids(position, ends):
    return jnp.sum((ends[None, :] <= position[:, None]).astype(jnp.int32), axis=1)


def document_ends(lengths):
    index = jnp.arange(lengths.shape[0])
    return jnp.sum(jnp.where(index[None, :] <= index[:, None], lengths[None, :], 0), axis=1)


def contract_rows(left, right):
    return lax.dot_general(
        left, right, (((0,), (0,)), ((), ())), preferred_element_type=jnp.float32
    )


def contract_cols(left, right):
    return lax.dot_general(
        left, right, (((1,), (1,)), ((), ())), preferred_element_type=jnp.float32
    )


def by_rings(layer_input, query_rows, key_rows, value_rows, grad_out, doc_lengths, block_order):
    rows = query_rows.shape[1]
    width = key_rows.shape[2]
    heads = query_rows.shape[2] // width
    parts = lax.axis_size("ctx")
    me = lax.axis_index("ctx")
    scale = width ** (-0.5)
    ends = document_ends(doc_lengths[0])
    queries = query_rows[0].reshape(rows * heads, width)
    grads = grad_out[0].reshape(rows * heads, width)
    own_pos = shard_positions(block_order, me, rows)
    query_pos = jnp.repeat(own_pos, heads)
    query_doc = jnp.repeat(document_ids(own_pos, ends), heads)
    paired = jnp.concatenate([key_rows[0], value_rows[0]], axis=1)
    query_zero = jnp.zeros((rows * heads, width), jnp.float32)
    pair_zero = jnp.zeros((rows, 2 * width), jnp.float32)

    def allowed_for(owner):
        key_pos = shard_positions(block_order, owner, rows)
        key_doc = document_ids(key_pos, ends)
        return (query_doc[:, None] == key_doc[None, :]) & (key_pos[None, :] <= query_pos[:, None])

    def forward_terms(state, block, allowed):
        best, total, weighted = state
        scores = contract_cols(queries, block[:, :width]) * scale
        masked = jnp.where(allowed, scores, -jnp.inf)
        new_best = jnp.maximum(best, jnp.max(masked, axis=1))
        safe_best = jnp.where(jnp.isfinite(new_best), new_best, 0.0)
        probs = jnp.where(allowed, jnp.exp(masked - safe_best[:, None]), 0.0)
        dprobs = contract_cols(grads, block[:, width:])
        factor = jnp.exp(best - safe_best)
        return (
            new_best,
            total * factor + jnp.sum(probs, axis=1),
            weighted * factor + jnp.sum(probs * dprobs, axis=1),
        )

    def forward_step(state, block, owner):
        allowed = allowed_for(owner)
        return forward_terms(state, block, allowed)

    def backward_terms(block, allowed, lse, delta):
        scores = contract_cols(queries, block[:, :width]) * scale
        probs = jnp.where(allowed, jnp.exp(scores - lse[:, None]), 0.0)
        dprobs = contract_cols(grads, block[:, width:])
        dscores = (probs * (dprobs - delta[:, None])).astype(jnp.bfloat16)
        weights = probs.astype(jnp.bfloat16)
        dquery = jnp.dot(dscores, block[:, :width], preferred_element_type=jnp.float32)
        dpair = jnp.concatenate(
            [contract_rows(dscores, queries), contract_rows(weights, grads)], axis=1
        )
        return (dquery, dpair)

    def backward_step(block, owner, lse, delta):
        allowed = allowed_for(owner)
        return backward_terms(block, allowed, lse, delta)

    start_state = (
        jnp.full((rows * heads,), -jnp.inf, jnp.float32),
        jnp.zeros((rows * heads,), jnp.float32),
        jnp.zeros((rows * heads,), jnp.float32),
    )

    def forward_turn(turn, carry):
        state, block = carry
        state = forward_step(state, block, (me - turn) % parts)
        block = passed_along(block, "ctx", 1)
        return (state, block)

    state, block = lax.fori_loop(0, parts - 1, forward_turn, (start_state, paired))
    best, total, weighted = forward_step(state, block, (me + 1) % parts)
    lse = best + jnp.log(total)
    delta = weighted / total

    def backward_turn(turn, carry):
        block, pair_grad, dquery = carry
        add_query, add_pair = backward_step(block, (me - turn) % parts, lse, delta)
        pair_grad = passed_along((pair_grad + add_pair).astype(jnp.bfloat16), "ctx", 1).astype(
            jnp.float32
        )
        block = passed_along(block, "ctx", 1)
        return (block, pair_grad, dquery + add_query)

    block, pair_grad, dquery = lax.fori_loop(
        0, parts, backward_turn, (paired, pair_zero, query_zero)
    )
    column = jnp.where(jnp.arange(2 * width) < width, scale, 1.0)
    pair_low = (pair_grad * column[None, :]).astype(jnp.bfloat16)
    inputs = layer_input[0]
    summed = lax.psum_scatter(
        contract_rows(inputs, pair_low), ("dp", "ctx"), scatter_dimension=0, tiled=True
    )
    grad_scale = (lax.axis_size("dp") * rows * parts) ** (-0.5)
    weight_grad = (summed * grad_scale).astype(jnp.bfloat16)
    query_grad = (dquery * scale).astype(jnp.bfloat16).reshape(1, rows, heads * width)
    return (query_grad, weight_grad)


def kernel(
    grad_scale, x_ref, q_ref, k_ref, v_ref, g_ref, len_hbm, order_hbm, dq_ref, dw_ref,
    len_ref, order_ref, load_sem, qs, gs, kbuf, vbuf, probs, dprobs, dscores, part, landed, pair, xa, xb,
    early, cross, crossed, zsum, zout, zland,
    k_send, k_recv, v_send, v_recv, x_send, x_recv, own_sem, part_send, part_recv,
    pair_send, pair_recv, cross_send, cross_recv, z_send, z_recv,
):
    rows, width = k_ref.shape
    heads = q_ref.shape[1] // width
    half = rows // 2
    lanes = rows * heads
    chunk = dw_ref.shape[0]
    parts = 4
    dp, me = lax.axis_index("dp"), lax.axis_index("ctx")
    y, x, c = dp // 4, (dp // 2) % 2, dp % 2

    def place(yy, xx, cc):
        return (yy * 2 + xx) * 2 + cc

    def remote(source, target, send, recv, where):
        return pltpu.make_async_remote_copy(
            src_ref=source, dst_ref=target, send_sem=send, recv_sem=recv,
            device_id=where, device_id_type=pl.DeviceIdType.MESH,
        )

    peers = [(dp, (me + s) % parts) for s in range(1, parts)]
    near = [
        (y, x, 1 - c), (y, 1 - x, c), (y, 1 - x, 1 - c), (1 - y, x, c), (1 - y, x, 1 - c),
    ]
    close = [(place(*n), me) for n in near]

    barrier = pltpu.get_barrier_semaphore()
    for where in peers + close:
        pl.semaphore_signal(barrier, inc=1, device_id=where, device_id_type=pl.DeviceIdType.MESH)

    loads = [
        (order_hbm, order_ref), (len_hbm, len_ref), (k_ref, kbuf.at[0]), (v_ref, vbuf.at[0]),
    ]
    for source, target in ((q_ref, qs), (g_ref, gs)):
        for h in range(heads):
            loads.append((source.at[:, pl.ds(h * width, width)], target.at[pl.ds(h * rows, rows), :]))
    loads = [pltpu.make_async_copy(a, b, load_sem.at[n]) for n, (a, b) in enumerate(loads)]
    for copy in loads:
        copy.start()

    pl.semaphore_wait(barrier, len(peers) + len(close))

    sent, kcopies, vcopies = [], [None], [None]
    for s in range(1, parts):
        where = peers[s - 1]
        kcopies.append(remote(k_ref, kbuf.at[s], k_send.at[s], k_recv.at[s], where))
        vcopies.append(remote(v_ref, vbuf.at[s], v_send.at[s], v_recv.at[s], where))
    for s in (1, 3, 2):
        kcopies[s].start()
        vcopies[s].start()
    sent += kcopies[1:] + vcopies[1:]

    xcopies, owned = [], []
    for slot, (cx, cc) in enumerate([(x, c), (x, 1 - c), (1 - x, c), (1 - x, 1 - c)]):
        for t in range(2):
            first = pl.multiple_of(place(t, cx, cc) * (parts * chunk), parts * chunk)
            source = x_ref.at[:, pl.ds(first, 2 * chunk)]
            target = xa.at[t, pl.ds(slot * rows, rows), :]
            if slot == 0:
                owned.append(pltpu.make_async_copy(source, target, own_sem.at[t]))
            else:
                n = slot * 2 + t
                xcopies.append(remote(source, target, x_send.at[0, n], x_recv.at[0, n], (place(y, cx, cc), me)))
    for slot, (cy, cc) in enumerate([(y, c), (y, 1 - c), (1 - y, c), (1 - y, 1 - c)]):
        for t in range(2):
            first = pl.multiple_of(place(cy, t, cc) * (parts * chunk) + 2 * chunk, 2 * chunk)
            source = x_ref.at[:, pl.ds(first, 2 * chunk)]
            target = xb.at[t, pl.ds(slot * rows, rows), :]
            if slot == 0:
                owned.append(pltpu.make_async_copy(source, target, own_sem.at[2 + t]))
            else:
                n = slot * 2 + t
                xcopies.append(remote(source, target, x_send.at[1, n], x_recv.at[1, n], (place(cy, x, cc), me)))
    for copy in xcopies + owned:
        copy.start()
    sent += xcopies

    for copy in loads[:2]:
        copy.wait()

    lane = lax.broadcasted_iota(jnp.int32, (1, lanes), 1)
    inside = lane
    for h in range(1, heads):
        inside = inside - jnp.where(lane >= h * rows, rows, 0)
    first = (order_ref[2 * me]) * half
    second = (order_ref[2 * me + 1] - 1) * half
    qpos = inside + jnp.where(inside < half, first, second)
    begin = jnp.zeros((1, lanes), jnp.int32)
    end = jnp.int32(0)
    for j in range(len_ref.shape[1]):
        end = end + len_ref[0, j]
        begin = jnp.where(qpos >= end, end, begin)
    row = lax.broadcasted_iota(jnp.int32, (rows, 1), 0)

    def nt(left, right):
        return lax.dot_general(left, right, (((1,), (1,)), ((), ())), preferred_element_type=jnp.float32)

    def nn(left, right):
        return jnp.dot(left, right, preferred_element_type=jnp.float32)

    scale = width ** (-0.5)
    base2 = scale * math.log2(math.e)
    order = (0, 1, 3, 2)
    for copy in loads[2:]:
        copy.wait()
    tops, sums, dots = {}, {}, {}
    for s in order:
        if s:
            kcopies[s].wait_recv()
            vcopies[s].wait_recv()
        owner = (me - s + parts) % parts
        one = (order_ref[2 * owner]) * half
        two = (order_ref[2 * owner + 1] - 1) * half
        kpos = row + jnp.where(row < half, one, two)
        allowed = (kpos >= begin) & (kpos <= qpos)
        scores = jnp.where(allowed, nt(kbuf[s], qs[...]) * base2, -1e30)
        tops[s] = jnp.max(scores, axis=0, keepdims=True)
        prob = jnp.exp2(scores - tops[s])
        dprob = nt(vbuf[s], gs[...])
        probs[s] = prob
        dprobs[s] = dprob
        sums[s] = jnp.sum(prob, axis=0, keepdims=True)
        dots[s] = jnp.sum(prob * dprob, axis=0, keepdims=True)
    best = jnp.maximum(jnp.maximum(tops[0], tops[1]), jnp.maximum(tops[2], tops[3]))
    gains = {s: jnp.exp2(tops[s] - best) for s in order}
    inverse = 1.0 / sum(sums[s] * gains[s] for s in order)
    delta = sum(dots[s] * gains[s] for s in order) * inverse

    partcopies = [None]
    for s in range(1, parts):
        where = (dp, (me - s + parts) % parts)
        partcopies.append(remote(part.at[s], landed.at[s], part_send.at[s], part_recv.at[s], where))
    own_pair = None
    for s in (2, 1, 3, 0):
        prob = probs[s] * (gains[s] * inverse)
        dscore = (prob * (dprobs[s] - delta)).astype(jnp.bfloat16)
        dscores[s * rows:(s + 1) * rows, :] = dscore
        dkey = nn(dscore, qs[...])
        dvalue = nn(prob.astype(jnp.bfloat16), gs[...])
        if s:
            part[s, :, :width] = dkey.astype(jnp.bfloat16)
            part[s, :, width:] = dvalue.astype(jnp.bfloat16)
            partcopies[s].start()
        else:
            own_pair = (dkey, dvalue)
    sent += partcopies[1:]

    keys = kbuf[...].reshape(parts * rows, width)
    dquery = nn(keys.T, dscores[...]) * scale
    for h in range(heads):
        dq_ref[:, h * width:(h + 1) * width] = (
            dquery[:, h * rows:(h + 1) * rows].T.astype(jnp.bfloat16)
        )

    dkey, dvalue = own_pair
    for s in (1, 3, 2):
        partcopies[s].wait_recv()
        dkey = dkey + landed[s, :, :width].astype(jnp.float32)
        dvalue = dvalue + landed[s, :, width:].astype(jnp.float32)
    pair[0:rows, :width] = (dkey * scale).astype(jnp.bfloat16)
    pair[0:rows, width:] = dvalue.astype(jnp.bfloat16)
    paircopies = [None]
    for n in range(1, 6):
        copy = remote(
            pair.at[pl.ds(0, rows), :], pair.at[pl.ds(n * rows, rows), :],
            pair_send.at[n], pair_recv.at[n], close[n - 1],
        )
        paircopies.append(copy)
    for n in (3, 5, 2, 4, 1):
        paircopies[n].start()
    sent += paircopies[1:]

    for copy in owned:
        copy.wait()
    for copy in xcopies:
        copy.wait_recv()
    paircopies[1].wait_recv()
    turned = pair[0:2 * rows, :].T
    for t in range(2):
        early[0, t] = nn(turned, xa[t, 0:2 * rows, :])
        early[1, t] = nn(turned, xb[t, 0:2 * rows, :])
    crosscopies = [[], []]
    kept = (y, x)
    away = [(place(1 - y, x, c), me), (place(y, 1 - x, c), me)]
    for a in range(2):
        for z in range(2):
            crosscopies[a].append(remote(
                cross.at[a, z], crossed.at[a, z], cross_send.at[a, z], cross_recv.at[a, z], away[a],
            ))
    turns = []
    for a, xs in enumerate((xa, xb)):
        paircopies[2 + 2 * a].wait_recv()
        paircopies[3 + 2 * a].wait_recv()
        turned = pair[(2 + 2 * a) * rows:(4 + 2 * a) * rows, :].T
        turns.append(turned)
        other = 1 - kept[a]
        for z in range(2):
            cols = slice(z * chunk, (z + 1) * chunk)
            made = early[a, other, :, cols] + nn(turned, xs[other, 2 * rows:4 * rows, cols])
            cross[a, z] = made.astype(jnp.bfloat16)
            crosscopies[a][z].start()
    for a, xs in enumerate((xa, xb)):
        for z in range(2):
            cols = slice(z * chunk, (z + 1) * chunk)
            zsum[2 * a + z] = early[a, kept[a], :, cols] + nn(turns[a], xs[kept[a], 2 * rows:4 * rows, cols])
        sent += crosscopies[a]

    for z, a in ((0, 0), (1, 0), (0, 1), (1, 1)):
        t = 2 * a + z
        crosscopies[a][z].wait_recv()
        made = zsum[t] + crossed[a, z].astype(jnp.float32)
        zsum[t] = made
        zout[t] = made.astype(jnp.bfloat16)

        @pl.when(me != t)
        def _():
            s = (t - me + parts) % parts
            remote(zout.at[t], zland.at[s], z_send.at[s], z_recv.at[s], (dp, t)).start()

    final = zsum[me]
    for s in (1, 3, 2):
        to = (me + s) % parts
        copy = remote(zout.at[to], zland.at[s], z_send.at[s], z_recv.at[s], (dp, to))
        copy.wait_recv()
        final = final + zland[s].astype(jnp.float32)
        sent.append(copy)
    dw_ref[...] = (final * grad_scale).T.astype(jnp.bfloat16)
    for copy in sent:
        copy.wait_send()


def fused(layer_input, query_rows, key_rows, value_rows, grad_out, doc_lengths, block_order):
    rows, width = key_rows.shape[1:]
    model = layer_input.shape[2]
    heads = query_rows.shape[2] // width
    count, parts = lax.axis_size("dp"), lax.axis_size("ctx")
    chunk = model // (count * parts)
    lanes = rows * heads
    grad_scale = (count * rows * parts) ** (-0.5)
    low, full = jnp.bfloat16, jnp.float32
    vmem = pl.BlockSpec(memory_space=pltpu.VMEM)
    dma = pltpu.SemaphoreType.DMA

    def body(*refs):
        kernel(grad_scale, *refs)

    query_grad, weight_grad = pl.pallas_call(
        body,
        out_shape=(
            jax.ShapeDtypeStruct((rows, heads * width), low),
            jax.ShapeDtypeStruct((chunk, 2 * width), low),
        ),
        in_specs=[pl.BlockSpec(memory_space=pltpu.HBM)] * 7,
        out_specs=(vmem, vmem),
        scratch_shapes=[
            pltpu.SMEM(doc_lengths.shape, jnp.int32),
            pltpu.SMEM(block_order.shape, jnp.int32),
            dma((4 + 2 * heads,)),
            pltpu.VMEM((lanes, width), low),
            pltpu.VMEM((lanes, width), low),
            pltpu.VMEM((parts, rows, width), low),
            pltpu.VMEM((parts, rows, width), low),
            pltpu.VMEM((parts, rows, lanes), full),
            pltpu.VMEM((parts, rows, lanes), full),
            pltpu.VMEM((parts * rows, lanes), low),
            pltpu.VMEM((parts, rows, 2 * width), low),
            pltpu.VMEM((parts, rows, 2 * width), low),
            pltpu.VMEM((6 * rows, 2 * width), low),
            pltpu.VMEM((2, 4 * rows, 2 * chunk), low),
            pltpu.VMEM((2, 4 * rows, 2 * chunk), low),
            pltpu.VMEM((2, 2, 2 * width, 2 * chunk), full),
            pltpu.VMEM((2, 2, 2 * width, chunk), low),
            pltpu.VMEM((2, 2, 2 * width, chunk), low),
            pltpu.VMEM((4, 2 * width, chunk), full),
            pltpu.VMEM((4, 2 * width, chunk), low),
            pltpu.VMEM((4, 2 * width, chunk), low),
            dma((4,)), dma((4,)), dma((4,)), dma((4,)),
            dma((2, 8)), dma((2, 8)), dma((4,)),
            dma((4,)), dma((4,)), dma((6,)), dma((6,)),
            dma((2, 2)), dma((2, 2)), dma((4,)), dma((4,)),
        ],
        compiler_params=pltpu.CompilerParams(
            collective_id=0, has_side_effects=True, vmem_limit_bytes=60 * 1024 * 1024
        ),
    )(layer_input[0], query_rows[0], key_rows[0], value_rows[0], grad_out[0], doc_lengths, block_order)
    return (query_grad[None], weight_grad)


def solution(mesh):
    placed = (
        P("dp", "ctx", None),
        P("dp", "ctx", None),
        P("dp", "ctx", None),
        P("dp", "ctx", None),
        P("dp", "ctx", None),
        P("dp", None),
        P(),
    )
    return jax.shard_map(
        fused if dict(mesh.shape) == {"dp": 8, "ctx": 4} else by_rings,
        mesh=mesh,
        in_specs=placed,
        out_specs=(P("dp", "ctx", None), P(("dp", "ctx"), None)),
        check_vma=False,
    )
```

```python
import math

import jax
import jax.numpy as jnp
from jax import lax
from jax.experimental import pallas as pl
from jax.experimental.pallas import tpu as pltpu
from jax.sharding import PartitionSpec as P


def passed_along(value, axis, steps):
    count = lax.axis_size(axis)
    pairs = [(source, (source + steps) % count) for source in range(count)]
    return lax.ppermute(value, axis, pairs)


def shard_positions(block_order, owner, rows):
    half = rows // 2
    local = jnp.arange(rows, dtype=jnp.int32)
    first = lax.dynamic_index_in_dim(block_order, 2 * owner, 0, keepdims=False)
    second = lax.dynamic_index_in_dim(block_order, 2 * owner + 1, 0, keepdims=False)
    blocks = jnp.where(local < half, first, second)
    return blocks * half + local % half


def document_ids(position, ends):
    return jnp.sum((ends[None, :] <= position[:, None]).astype(jnp.int32), axis=1)


def document_ends(lengths):
    index = jnp.arange(lengths.shape[0])
    return jnp.sum(jnp.where(index[None, :] <= index[:, None], lengths[None, :], 0), axis=1)


def contract_rows(left, right):
    return lax.dot_general(
        left, right, (((0,), (0,)), ((), ())), preferred_element_type=jnp.float32
    )


def contract_cols(left, right):
    return lax.dot_general(
        left, right, (((1,), (1,)), ((), ())), preferred_element_type=jnp.float32
    )


def by_rings(layer_input, query_rows, key_rows, value_rows, grad_out, doc_lengths, block_order):
    rows = query_rows.shape[1]
    width = key_rows.shape[2]
    heads = query_rows.shape[2] // width
    parts = lax.axis_size("ctx")
    me = lax.axis_index("ctx")
    scale = width ** (-0.5)
    ends = document_ends(doc_lengths[0])
    queries = query_rows[0].reshape(rows * heads, width)
    grads = grad_out[0].reshape(rows * heads, width)
    own_pos = shard_positions(block_order, me, rows)
    query_pos = jnp.repeat(own_pos, heads)
    query_doc = jnp.repeat(document_ids(own_pos, ends), heads)
    paired = jnp.concatenate([key_rows[0], value_rows[0]], axis=1)
    query_zero = jnp.zeros((rows * heads, width), jnp.float32)
    pair_zero = jnp.zeros((rows, 2 * width), jnp.float32)

    def allowed_for(owner):
        key_pos = shard_positions(block_order, owner, rows)
        key_doc = document_ids(key_pos, ends)
        return (query_doc[:, None] == key_doc[None, :]) & (key_pos[None, :] <= query_pos[:, None])

    def forward_terms(state, block, allowed):
        best, total, weighted = state
        scores = contract_cols(queries, block[:, :width]) * scale
        masked = jnp.where(allowed, scores, -jnp.inf)
        new_best = jnp.maximum(best, jnp.max(masked, axis=1))
        safe_best = jnp.where(jnp.isfinite(new_best), new_best, 0.0)
        probs = jnp.where(allowed, jnp.exp(masked - safe_best[:, None]), 0.0)
        dprobs = contract_cols(grads, block[:, width:])
        factor = jnp.exp(best - safe_best)
        return (
            new_best,
            total * factor + jnp.sum(probs, axis=1),
            weighted * factor + jnp.sum(probs * dprobs, axis=1),
        )

    def forward_step(state, block, owner):
        allowed = allowed_for(owner)
        return forward_terms(state, block, allowed)

    def backward_terms(block, allowed, lse, delta):
        scores = contract_cols(queries, block[:, :width]) * scale
        probs = jnp.where(allowed, jnp.exp(scores - lse[:, None]), 0.0)
        dprobs = contract_cols(grads, block[:, width:])
        dscores = (probs * (dprobs - delta[:, None])).astype(jnp.bfloat16)
        weights = probs.astype(jnp.bfloat16)
        dquery = jnp.dot(dscores, block[:, :width], preferred_element_type=jnp.float32)
        dpair = jnp.concatenate(
            [contract_rows(dscores, queries), contract_rows(weights, grads)], axis=1
        )
        return (dquery, dpair)

    def backward_step(block, owner, lse, delta):
        allowed = allowed_for(owner)
        return backward_terms(block, allowed, lse, delta)

    start_state = (
        jnp.full((rows * heads,), -jnp.inf, jnp.float32),
        jnp.zeros((rows * heads,), jnp.float32),
        jnp.zeros((rows * heads,), jnp.float32),
    )

    def forward_turn(turn, carry):
        state, block = carry
        state = forward_step(state, block, (me - turn) % parts)
        block = passed_along(block, "ctx", 1)
        return (state, block)

    state, block = lax.fori_loop(0, parts - 1, forward_turn, (start_state, paired))
    best, total, weighted = forward_step(state, block, (me + 1) % parts)
    lse = best + jnp.log(total)
    delta = weighted / total

    def backward_turn(turn, carry):
        block, pair_grad, dquery = carry
        add_query, add_pair = backward_step(block, (me - turn) % parts, lse, delta)
        pair_grad = passed_along((pair_grad + add_pair).astype(jnp.bfloat16), "ctx", 1).astype(
            jnp.float32
        )
        block = passed_along(block, "ctx", 1)
        return (block, pair_grad, dquery + add_query)

    block, pair_grad, dquery = lax.fori_loop(
        0, parts, backward_turn, (paired, pair_zero, query_zero)
    )
    column = jnp.where(jnp.arange(2 * width) < width, scale, 1.0)
    pair_low = (pair_grad * column[None, :]).astype(jnp.bfloat16)
    inputs = layer_input[0]
    summed = lax.psum_scatter(
        contract_rows(inputs, pair_low), ("dp", "ctx"), scatter_dimension=0, tiled=True
    )
    grad_scale = (lax.axis_size("dp") * rows * parts) ** (-0.5)
    weight_grad = (summed * grad_scale).astype(jnp.bfloat16)
    query_grad = (dquery * scale).astype(jnp.bfloat16).reshape(1, rows, heads * width)
    return (query_grad, weight_grad)


def kernel(
    grad_scale, x_ref, q_ref, k_ref, v_ref, g_ref, len_hbm, order_hbm, dq_ref, dw_ref,
    len_ref, order_ref, load_sem, qs, gs, kbuf, vbuf, probs, dprobs, dscores, part, landed, total_pair, pair, xa, xb,
    early, cross, crossed, zsum, zout, zland,
    k_send, k_recv, v_send, v_recv, x_send, x_recv, own_sem, part_send, part_recv,
    pair_send, pair_recv, cross_send, cross_recv, z_send, z_recv,
):
    rows, width = k_ref.shape
    heads = q_ref.shape[1] // width
    half = rows // 2
    lanes = rows * heads
    chunk = dw_ref.shape[0]
    parts = 4
    dp, me = lax.axis_index("dp"), lax.axis_index("ctx")
    y, x, c = dp // 4, (dp // 2) % 2, dp % 2

    def place(yy, xx, cc):
        return (yy * 2 + xx) * 2 + cc

    def remote(source, target, send, recv, where):
        return pltpu.make_async_remote_copy(
            src_ref=source, dst_ref=target, send_sem=send, recv_sem=recv,
            device_id=where, device_id_type=pl.DeviceIdType.MESH,
        )

    peers = [(dp, (me + s) % parts) for s in range(1, parts)]
    near = [
        (y, x, 1 - c), (y, 1 - x, c), (y, 1 - x, 1 - c), (1 - y, x, c), (1 - y, x, 1 - c),
    ]
    close = [(place(*n), me) for n in near]

    barrier = pltpu.get_barrier_semaphore()
    for where in peers + close:
        pl.semaphore_signal(barrier, inc=1, device_id=where, device_id_type=pl.DeviceIdType.MESH)

    loads = [
        (order_hbm, order_ref), (len_hbm, len_ref), (k_ref, kbuf.at[0]), (v_ref, vbuf.at[0]),
    ]
    for source, target in ((q_ref, qs), (g_ref, gs)):
        for h in range(heads):
            loads.append((source.at[:, pl.ds(h * width, width)], target.at[pl.ds(h * rows, rows), :]))
    loads = [pltpu.make_async_copy(a, b, load_sem.at[n]) for n, (a, b) in enumerate(loads)]
    for copy in loads:
        copy.start()

    pl.semaphore_wait(barrier, len(peers) + len(close))

    sent, kcopies, vcopies = [], [None], [None]
    for s in range(1, parts):
        where = peers[s - 1]
        kcopies.append(remote(k_ref, kbuf.at[s], k_send.at[s], k_recv.at[s], where))
        vcopies.append(remote(v_ref, vbuf.at[s], v_send.at[s], v_recv.at[s], where))
    last = parts - 1
    ends = (me == 0) | (me == last)
    skipped = jnp.where(me == 0, last, 1)
    kcopies[2].start()
    vcopies[2].start()
    for s in (1, 3):
        @pl.when(jnp.logical_not(ends & (skipped == s)))
        def _(s=s):
            kcopies[s].start()
            vcopies[s].start()
    far = jnp.where(me == 1, 0, last)
    relay_slot = jnp.where(me == 1, 1, last)
    relays = [
        remote(kbuf.at[2], kbuf.at[relay_slot], k_send.at[0], k_recv.at[relay_slot], (dp, far)),
        remote(vbuf.at[2], vbuf.at[relay_slot], v_send.at[0], v_recv.at[relay_slot], (dp, far)),
    ]

    xcopies, owned = [], []
    for slot, (cx, cc) in enumerate([(x, c), (x, 1 - c), (1 - x, c), (1 - x, 1 - c)]):
        for t in range(2):
            first = pl.multiple_of(place(t, cx, cc) * (parts * chunk), parts * chunk)
            source = x_ref.at[:, pl.ds(first, 2 * chunk)]
            target = xa.at[t, pl.ds(slot * rows, rows), :]
            if slot == 0:
                owned.append(pltpu.make_async_copy(source, target, own_sem.at[t]))
            else:
                n = slot * 2 + t
                xcopies.append(remote(source, target, x_send.at[0, n], x_recv.at[0, n], (place(y, cx, cc), me)))
    for slot, (cy, cc) in enumerate([(y, c), (y, 1 - c), (1 - y, c), (1 - y, 1 - c)]):
        for t in range(2):
            first = pl.multiple_of(place(cy, t, cc) * (parts * chunk) + 2 * chunk, 2 * chunk)
            source = x_ref.at[:, pl.ds(first, 2 * chunk)]
            target = xb.at[t, pl.ds(slot * rows, rows), :]
            if slot == 0:
                owned.append(pltpu.make_async_copy(source, target, own_sem.at[2 + t]))
            else:
                n = slot * 2 + t
                xcopies.append(remote(source, target, x_send.at[1, n], x_recv.at[1, n], (place(cy, x, cc), me)))
    for copy in xcopies + owned:
        copy.start()
    sent += xcopies

    for copy in loads[:2]:
        copy.wait()

    lane = lax.broadcasted_iota(jnp.int32, (1, lanes), 1)
    inside = lane
    for h in range(1, heads):
        inside = inside - jnp.where(lane >= h * rows, rows, 0)
    first = (order_ref[2 * me]) * half
    second = (order_ref[2 * me + 1] - 1) * half
    qpos = inside + jnp.where(inside < half, first, second)
    begin = jnp.zeros((1, lanes), jnp.int32)
    end = jnp.int32(0)
    for j in range(len_ref.shape[1]):
        end = end + len_ref[0, j]
        begin = jnp.where(qpos >= end, end, begin)
    row = lax.broadcasted_iota(jnp.int32, (rows, 1), 0)

    def nt(left, right):
        return lax.dot_general(left, right, (((1,), (1,)), ((), ())), preferred_element_type=jnp.float32)

    def nn(left, right):
        return jnp.dot(left, right, preferred_element_type=jnp.float32)

    scale = width ** (-0.5)
    base2 = scale * math.log2(math.e)
    for copy in loads[2:]:
        copy.wait()
    tops, sums, dots = {}, {}, {}
    near_slot = jnp.where(me == 0, last, 1)
    slots = [
        0, jnp.where(ends, 2, 1), jnp.where(ends, near_slot, 2), jnp.where(ends, parts - near_slot, 3),
    ]
    order = range(parts)

    def arrived(n):
        to = (dp, (me + n) % parts)
        remote(k_ref, kbuf.at[n], k_send.at[n], k_recv.at[n], to).wait_recv()
        remote(v_ref, vbuf.at[n], v_send.at[n], v_recv.at[n], to).wait_recv()

    for s, slot in enumerate(slots):
        if s == 1:
            arrived(2)

            @pl.when(jnp.logical_not(ends))
            def _():
                for copy in relays:
                    copy.start()
                arrived(1)
        elif s == 2:
            @pl.when(ends)
            def _():
                arrived(near_slot)
        elif s == 3:
            arrived(slots[3])
        owner = (me - slot + parts) % parts
        one = (order_ref[2 * owner]) * half
        two = (order_ref[2 * owner + 1] - 1) * half
        kpos = row + jnp.where(row < half, one, two)
        allowed = (kpos >= begin) & (kpos <= qpos)
        scores = jnp.where(allowed, nt(kbuf[slot], qs[...]) * base2, -1e30)
        tops[s] = jnp.max(scores, axis=0, keepdims=True)
        prob = jnp.exp2(scores - tops[s])
        dprob = nt(vbuf[slot], gs[...])
        probs[s] = prob
        dprobs[s] = dprob
        sums[s] = jnp.sum(prob, axis=0, keepdims=True)
        dots[s] = jnp.sum(prob * dprob, axis=0, keepdims=True)
    best = jnp.maximum(jnp.maximum(tops[0], tops[1]), jnp.maximum(tops[2], tops[3]))
    gains = {s: jnp.exp2(tops[s] - best) for s in order}
    inverse = 1.0 / sum(sums[s] * gains[s] for s in order)
    delta = sum(dots[s] * gains[s] for s in order) * inverse

    beside = jnp.where(me == 0, 1, 2)
    routes = {
        3: (jnp.where(ends, beside, (me + 1) % parts), jnp.where(ends, 0, 3)),
        1: ((me - slots[1] + parts) % parts, slots[1]),
        2: ((me - slots[2] + parts) % parts, slots[2]),
    }
    partcopies = {
        p: remote(part.at[p], landed.at[to], part_send.at[p], part_recv.at[to], (dp, device))
        for p, (device, to) in routes.items()
    }
    handed = remote(part.at[3], landed.at[0], part_send.at[3], part_recv.at[0], (dp, beside))

    @pl.when(ends)
    def _():
        landed[near_slot] = jnp.zeros(landed.shape[1:], landed.dtype)

    own_pair = None
    for s in (3, 1, 2, 0):
        prob = probs[s] * (gains[s] * inverse)
        dscore = (prob * (dprobs[s] - delta)).astype(jnp.bfloat16)
        dscores[s * rows:(s + 1) * rows, :] = dscore
        dkey = nn(dscore, qs[...])
        dvalue = nn(prob.astype(jnp.bfloat16), gs[...])
        if s in (3, 1):
            part[s, :, :width] = dkey.astype(jnp.bfloat16)
            part[s, :, width:] = dvalue.astype(jnp.bfloat16)
            partcopies[s].start()
        elif s == 2:
            total_pair[:, :width] = dkey
            total_pair[:, width:] = dvalue

            @pl.when(jnp.logical_not(ends))
            def _():
                handed.wait_recv()
                total_pair[...] += landed[0].astype(jnp.float32)

            part[2] = total_pair[...].astype(jnp.bfloat16)
            partcopies[2].start()
        else:
            own_pair = (dkey, dvalue)
    sent += list(partcopies.values())

    keys = jnp.concatenate([kbuf[slot] for slot in slots], axis=0)
    dquery = nn(keys.T, dscores[...]) * scale
    for h in range(heads):
        dq_ref[:, h * width:(h + 1) * width] = (
            dquery[:, h * rows:(h + 1) * rows].T.astype(jnp.bfloat16)
        )

    dkey, dvalue = own_pair
    def part_in(n):
        remote(part.at[n], landed.at[n], part_send.at[n], part_recv.at[n], (dp, (me + n) % parts)).wait_recv()

    pl.when(me != last)(lambda: part_in(1))
    pl.when(me != 0)(lambda: part_in(3))
    part_in(2)
    for s in (1, 3, 2):
        dkey = dkey + landed[s, :, :width].astype(jnp.float32)
        dvalue = dvalue + landed[s, :, width:].astype(jnp.float32)
    pair[0:rows, :width] = (dkey * scale).astype(jnp.bfloat16)
    pair[0:rows, width:] = dvalue.astype(jnp.bfloat16)
    paircopies = [None]
    for n in range(1, 6):
        copy = remote(
            pair.at[pl.ds(0, rows), :], pair.at[pl.ds(n * rows, rows), :],
            pair_send.at[n], pair_recv.at[n], close[n - 1],
        )
        paircopies.append(copy)
    for n in (3, 5, 2, 4, 1):
        paircopies[n].start()
    sent += paircopies[1:]

    for copy in owned:
        copy.wait()
    for copy in xcopies:
        copy.wait_recv()
    paircopies[1].wait_recv()
    turned = pair[0:2 * rows, :].T
    for t in range(2):
        early[0, t] = nn(turned, xa[t, 0:2 * rows, :])
        early[1, t] = nn(turned, xb[t, 0:2 * rows, :])
    crosscopies = [[], []]
    kept = (y, x)
    away = [(place(1 - y, x, c), me), (place(y, 1 - x, c), me)]
    for a in range(2):
        for z in range(2):
            crosscopies[a].append(remote(
                cross.at[a, z], crossed.at[a, z], cross_send.at[a, z], cross_recv.at[a, z], away[a],
            ))
    turns = []
    for a, xs in enumerate((xa, xb)):
        paircopies[2 + 2 * a].wait_recv()
        paircopies[3 + 2 * a].wait_recv()
        turned = pair[(2 + 2 * a) * rows:(4 + 2 * a) * rows, :].T
        turns.append(turned)
        other = 1 - kept[a]
        for z in range(2):
            cols = slice(z * chunk, (z + 1) * chunk)
            made = early[a, other, :, cols] + nn(turned, xs[other, 2 * rows:4 * rows, cols])
            cross[a, z] = made.astype(jnp.bfloat16)
            crosscopies[a][z].start()
    for a, xs in enumerate((xa, xb)):
        for z in range(2):
            cols = slice(z * chunk, (z + 1) * chunk)
            zsum[2 * a + z] = early[a, kept[a], :, cols] + nn(turns[a], xs[kept[a], 2 * rows:4 * rows, cols])
        sent += crosscopies[a]

    for z, a in ((0, 0), (1, 0), (0, 1), (1, 1)):
        t = 2 * a + z
        crosscopies[a][z].wait_recv()
        made = zsum[t] + crossed[a, z].astype(jnp.float32)
        zsum[t] = made
        zout[t] = made.astype(jnp.bfloat16)

        @pl.when(me != t)
        def _():
            s = (t - me + parts) % parts
            remote(zout.at[t], zland.at[s], z_send.at[s], z_recv.at[s], (dp, t)).start()

    final = zsum[me]
    for s in (1, 3, 2):
        to = (me + s) % parts
        copy = remote(zout.at[to], zland.at[s], z_send.at[s], z_recv.at[s], (dp, to))
        copy.wait_recv()
        final = final + zland[s].astype(jnp.float32)
        sent.append(copy)
    dw_ref[...] = (final * grad_scale).T.astype(jnp.bfloat16)
    kcopies[2].wait_send()
    vcopies[2].wait_send()
    for s in (1, 3):
        @pl.when(jnp.logical_not(ends & (skipped == s)))
        def _(s=s):
            kcopies[s].wait_send()
            vcopies[s].wait_send()

    @pl.when(jnp.logical_not(ends))
    def _():
        for copy in relays:
            copy.wait_send()

    for copy in sent:
        copy.wait_send()


def fused(layer_input, query_rows, key_rows, value_rows, grad_out, doc_lengths, block_order):
    rows, width = key_rows.shape[1:]
    model = layer_input.shape[2]
    heads = query_rows.shape[2] // width
    count, parts = lax.axis_size("dp"), lax.axis_size("ctx")
    chunk = model // (count * parts)
    lanes = rows * heads
    grad_scale = (count * rows * parts) ** (-0.5)
    low, full = jnp.bfloat16, jnp.float32
    vmem = pl.BlockSpec(memory_space=pltpu.VMEM)
    dma = pltpu.SemaphoreType.DMA

    def body(*refs):
        kernel(grad_scale, *refs)

    query_grad, weight_grad = pl.pallas_call(
        body,
        out_shape=(
            jax.ShapeDtypeStruct((rows, heads * width), low),
            jax.ShapeDtypeStruct((chunk, 2 * width), low),
        ),
        in_specs=[pl.BlockSpec(memory_space=pltpu.HBM)] * 7,
        out_specs=(vmem, vmem),
        scratch_shapes=[
            pltpu.SMEM(doc_lengths.shape, jnp.int32),
            pltpu.SMEM(block_order.shape, jnp.int32),
            dma((4 + 2 * heads,)),
            pltpu.VMEM((lanes, width), low),
            pltpu.VMEM((lanes, width), low),
            pltpu.VMEM((parts, rows, width), low),
            pltpu.VMEM((parts, rows, width), low),
            pltpu.VMEM((parts, rows, lanes), full),
            pltpu.VMEM((parts, rows, lanes), full),
            pltpu.VMEM((parts * rows, lanes), low),
            pltpu.VMEM((parts, rows, 2 * width), low),
            pltpu.VMEM((parts, rows, 2 * width), low),
            pltpu.VMEM((rows, 2 * width), full),
            pltpu.VMEM((6 * rows, 2 * width), low),
            pltpu.VMEM((2, 4 * rows, 2 * chunk), low),
            pltpu.VMEM((2, 4 * rows, 2 * chunk), low),
            pltpu.VMEM((2, 2, 2 * width, 2 * chunk), full),
            pltpu.VMEM((2, 2, 2 * width, chunk), low),
            pltpu.VMEM((2, 2, 2 * width, chunk), low),
            pltpu.VMEM((4, 2 * width, chunk), full),
            pltpu.VMEM((4, 2 * width, chunk), low),
            pltpu.VMEM((4, 2 * width, chunk), low),
            dma((4,)), dma((4,)), dma((4,)), dma((4,)),
            dma((2, 8)), dma((2, 8)), dma((4,)),
            dma((4,)), dma((4,)), dma((6,)), dma((6,)),
            dma((2, 2)), dma((2, 2)), dma((4,)), dma((4,)),
        ],
        compiler_params=pltpu.CompilerParams(
            collective_id=0, has_side_effects=True, vmem_limit_bytes=60 * 1024 * 1024
        ),
    )(layer_input[0], query_rows[0], key_rows[0], value_rows[0], grad_out[0], doc_lengths, block_order)
    return (query_grad[None], weight_grad)


def solution(mesh):
    placed = (
        P("dp", "ctx", None),
        P("dp", "ctx", None),
        P("dp", "ctx", None),
        P("dp", "ctx", None),
        P("dp", "ctx", None),
        P("dp", None),
        P(),
    )
    return jax.shard_map(
        fused if dict(mesh.shape) == {"dp": 8, "ctx": 4} else by_rings,
        mesh=mesh,
        in_specs=placed,
        out_specs=(P("dp", "ctx", None), P(("dp", "ctx"), None)),
        check_vma=False,
    )
```

```python
import math

import jax
import jax.numpy as jnp
from jax import lax
from jax.experimental import pallas as pl
from jax.experimental.pallas import tpu as pltpu
from jax.sharding import PartitionSpec as P


def passed_along(value, axis, steps):
    count = lax.axis_size(axis)
    pairs = [(source, (source + steps) % count) for source in range(count)]
    return lax.ppermute(value, axis, pairs)


def shard_positions(block_order, owner, rows):
    half = rows // 2
    local = jnp.arange(rows, dtype=jnp.int32)
    first = lax.dynamic_index_in_dim(block_order, 2 * owner, 0, keepdims=False)
    second = lax.dynamic_index_in_dim(block_order, 2 * owner + 1, 0, keepdims=False)
    blocks = jnp.where(local < half, first, second)
    return blocks * half + local % half


def document_ids(position, ends):
    return jnp.sum((ends[None, :] <= position[:, None]).astype(jnp.int32), axis=1)


def document_ends(lengths):
    index = jnp.arange(lengths.shape[0])
    return jnp.sum(jnp.where(index[None, :] <= index[:, None], lengths[None, :], 0), axis=1)


def contract_rows(left, right):
    return lax.dot_general(
        left, right, (((0,), (0,)), ((), ())), preferred_element_type=jnp.float32
    )


def contract_cols(left, right):
    return lax.dot_general(
        left, right, (((1,), (1,)), ((), ())), preferred_element_type=jnp.float32
    )


def by_rings(layer_input, query_rows, key_rows, value_rows, grad_out, doc_lengths, block_order):
    rows = query_rows.shape[1]
    width = key_rows.shape[2]
    heads = query_rows.shape[2] // width
    parts = lax.axis_size("ctx")
    me = lax.axis_index("ctx")
    scale = width ** (-0.5)
    ends = document_ends(doc_lengths[0])
    queries = query_rows[0].reshape(rows * heads, width)
    grads = grad_out[0].reshape(rows * heads, width)
    own_pos = shard_positions(block_order, me, rows)
    query_pos = jnp.repeat(own_pos, heads)
    query_doc = jnp.repeat(document_ids(own_pos, ends), heads)
    paired = jnp.concatenate([key_rows[0], value_rows[0]], axis=1)
    query_zero = jnp.zeros((rows * heads, width), jnp.float32)
    pair_zero = jnp.zeros((rows, 2 * width), jnp.float32)

    def allowed_for(owner):
        key_pos = shard_positions(block_order, owner, rows)
        key_doc = document_ids(key_pos, ends)
        return (query_doc[:, None] == key_doc[None, :]) & (key_pos[None, :] <= query_pos[:, None])

    def forward_terms(state, block, allowed):
        best, total, weighted = state
        scores = contract_cols(queries, block[:, :width]) * scale
        masked = jnp.where(allowed, scores, -jnp.inf)
        new_best = jnp.maximum(best, jnp.max(masked, axis=1))
        safe_best = jnp.where(jnp.isfinite(new_best), new_best, 0.0)
        probs = jnp.where(allowed, jnp.exp(masked - safe_best[:, None]), 0.0)
        dprobs = contract_cols(grads, block[:, width:])
        factor = jnp.exp(best - safe_best)
        return (
            new_best,
            total * factor + jnp.sum(probs, axis=1),
            weighted * factor + jnp.sum(probs * dprobs, axis=1),
        )

    def forward_step(state, block, owner):
        allowed = allowed_for(owner)
        return forward_terms(state, block, allowed)

    def backward_terms(block, allowed, lse, delta):
        scores = contract_cols(queries, block[:, :width]) * scale
        probs = jnp.where(allowed, jnp.exp(scores - lse[:, None]), 0.0)
        dprobs = contract_cols(grads, block[:, width:])
        dscores = (probs * (dprobs - delta[:, None])).astype(jnp.bfloat16)
        weights = probs.astype(jnp.bfloat16)
        dquery = jnp.dot(dscores, block[:, :width], preferred_element_type=jnp.float32)
        dpair = jnp.concatenate(
            [contract_rows(dscores, queries), contract_rows(weights, grads)], axis=1
        )
        return (dquery, dpair)

    def backward_step(block, owner, lse, delta):
        allowed = allowed_for(owner)
        return backward_terms(block, allowed, lse, delta)

    start_state = (
        jnp.full((rows * heads,), -jnp.inf, jnp.float32),
        jnp.zeros((rows * heads,), jnp.float32),
        jnp.zeros((rows * heads,), jnp.float32),
    )

    def forward_turn(turn, carry):
        state, block = carry
        state = forward_step(state, block, (me - turn) % parts)
        block = passed_along(block, "ctx", 1)
        return (state, block)

    state, block = lax.fori_loop(0, parts - 1, forward_turn, (start_state, paired))
    best, total, weighted = forward_step(state, block, (me + 1) % parts)
    lse = best + jnp.log(total)
    delta = weighted / total

    def backward_turn(turn, carry):
        block, pair_grad, dquery = carry
        add_query, add_pair = backward_step(block, (me - turn) % parts, lse, delta)
        pair_grad = passed_along((pair_grad + add_pair).astype(jnp.bfloat16), "ctx", 1).astype(
            jnp.float32
        )
        block = passed_along(block, "ctx", 1)
        return (block, pair_grad, dquery + add_query)

    block, pair_grad, dquery = lax.fori_loop(
        0, parts, backward_turn, (paired, pair_zero, query_zero)
    )
    column = jnp.where(jnp.arange(2 * width) < width, scale, 1.0)
    pair_low = (pair_grad * column[None, :]).astype(jnp.bfloat16)
    inputs = layer_input[0]
    summed = lax.psum_scatter(
        contract_rows(inputs, pair_low), ("dp", "ctx"), scatter_dimension=0, tiled=True
    )
    grad_scale = (lax.axis_size("dp") * rows * parts) ** (-0.5)
    weight_grad = (summed * grad_scale).astype(jnp.bfloat16)
    query_grad = (dquery * scale).astype(jnp.bfloat16).reshape(1, rows, heads * width)
    return (query_grad, weight_grad)


def kernel(
    grad_scale, x_ref, q_ref, k_ref, v_ref, g_ref, len_hbm, order_hbm, dq_ref, dw_ref,
    len_ref, order_ref, load_sem, qs, gs, kbuf, vbuf, probs, dprobs, dscores, part, landed, pair, xab, turned,
    early, cross, crossed, zsum, zout, zland,
    k_send, k_recv, v_send, v_recv, x_send, x_recv, own_sem, part_send, part_recv,
    pair_send, pair_recv, cross_send, cross_recv, z_send, z_recv,
):
    rows, width = k_ref.shape
    heads = q_ref.shape[1] // width
    half = rows // 2
    lanes = rows * heads
    chunk = dw_ref.shape[0]
    parts = 4
    dp, me = lax.axis_index("dp"), lax.axis_index("ctx")
    y, x, c = dp // 4, (dp // 2) % 2, dp % 2

    def place(yy, xx, cc):
        return (yy * 2 + xx) * 2 + cc

    def remote(source, target, send, recv, where):
        return pltpu.make_async_remote_copy(
            src_ref=source, dst_ref=target, send_sem=send, recv_sem=recv,
            device_id=where, device_id_type=pl.DeviceIdType.MESH,
        )

    peers = [(dp, (me + s) % parts) for s in range(1, parts)]
    near = [
        (y, x, 1 - c), (y, 1 - x, c), (y, 1 - x, 1 - c), (1 - y, x, c), (1 - y, x, 1 - c),
    ]
    close = [(place(*n), me) for n in near]

    barrier = pltpu.get_barrier_semaphore()
    for where in peers + close:
        pl.semaphore_signal(barrier, inc=1, device_id=where, device_id_type=pl.DeviceIdType.MESH)

    loads = [
        (order_hbm, order_ref), (len_hbm, len_ref), (k_ref, kbuf.at[0]), (v_ref, vbuf.at[0]),
    ]
    for source, target in ((q_ref, qs), (g_ref, gs)):
        for h in range(heads):
            loads.append((source.at[:, pl.ds(h * width, width)], target.at[pl.ds(h * rows, rows), :]))
    loads = [pltpu.make_async_copy(a, b, load_sem.at[n]) for n, (a, b) in enumerate(loads)]
    for copy in loads:
        copy.start()

    pl.semaphore_wait(barrier, len(peers) + len(close))

    sent, kcopies, vcopies = [], [None], [None]
    for s in range(1, parts):
        where = peers[s - 1]
        kcopies.append(remote(k_ref, kbuf.at[s], k_send.at[s], k_recv.at[s], where))
        vcopies.append(remote(v_ref, vbuf.at[s], v_send.at[s], v_recv.at[s], where))
    for s in (1, 3, 2):
        kcopies[s].start()
        vcopies[s].start()
    sent += kcopies[1:] + vcopies[1:]

    xcopies, owned = [], []
    for slot, (cx, cc) in enumerate([(x, c), (x, 1 - c), (1 - x, c), (1 - x, 1 - c)]):
        for t in range(2):
            first = pl.multiple_of(place(t, cx, cc) * (parts * chunk), parts * chunk)
            source = x_ref.at[:, pl.ds(first, 2 * chunk)]
            target = xab.at[0, t, pl.ds(slot * rows, rows), :]
            if slot == 0:
                owned.append(pltpu.make_async_copy(source, target, own_sem.at[t]))
            else:
                n = slot * 2 + t
                xcopies.append(remote(source, target, x_send.at[0, n], x_recv.at[0, n], (place(y, cx, cc), me)))
    for slot, (cy, cc) in enumerate([(y, c), (y, 1 - c), (1 - y, c), (1 - y, 1 - c)]):
        for t in range(2):
            first = pl.multiple_of(place(cy, t, cc) * (parts * chunk) + 2 * chunk, 2 * chunk)
            source = x_ref.at[:, pl.ds(first, 2 * chunk)]
            target = xab.at[1, t, pl.ds(slot * rows, rows), :]
            if slot == 0:
                owned.append(pltpu.make_async_copy(source, target, own_sem.at[2 + t]))
            else:
                n = slot * 2 + t
                xcopies.append(remote(source, target, x_send.at[1, n], x_recv.at[1, n], (place(cy, x, cc), me)))
    for copy in xcopies + owned:
        copy.start()
    sent += xcopies

    for copy in loads[:2]:
        copy.wait()

    lane = lax.broadcasted_iota(jnp.int32, (1, lanes), 1)
    inside = lane
    for h in range(1, heads):
        inside = inside - jnp.where(lane >= h * rows, rows, 0)
    first = (order_ref[2 * me]) * half
    second = (order_ref[2 * me + 1] - 1) * half
    qpos = inside + jnp.where(inside < half, first, second)
    begin = jnp.zeros((1, lanes), jnp.int32)
    end = jnp.int32(0)
    for j in range(len_ref.shape[1]):
        end = end + len_ref[0, j]
        begin = jnp.where(qpos >= end, end, begin)
    row = lax.broadcasted_iota(jnp.int32, (rows, 1), 0)

    def nt(left, right):
        return lax.dot_general(left, right, (((1,), (1,)), ((), ())), preferred_element_type=jnp.float32)

    def nn(left, right):
        return jnp.dot(left, right, preferred_element_type=jnp.float32)

    scale = width ** (-0.5)
    base2 = scale * math.log2(math.e)
    order = (0, 1, 3, 2)
    for copy in loads[2:]:
        copy.wait()
    tops, sums, dots = {}, {}, {}
    for s in order:
        if s:
            kcopies[s].wait_recv()
            vcopies[s].wait_recv()
        owner = (me - s + parts) % parts
        one = (order_ref[2 * owner]) * half
        two = (order_ref[2 * owner + 1] - 1) * half
        kpos = row + jnp.where(row < half, one, two)
        allowed = (kpos >= begin) & (kpos <= qpos)
        scores = jnp.where(allowed, nt(kbuf[s], qs[...]) * base2, -1e30)
        tops[s] = jnp.max(scores, axis=0, keepdims=True)
        prob = jnp.exp2(scores - tops[s])
        dprob = nt(vbuf[s], gs[...])
        probs[s] = prob
        dprobs[s] = dprob
        sums[s] = jnp.sum(prob, axis=0, keepdims=True)
        dots[s] = jnp.sum(prob * dprob, axis=0, keepdims=True)
    best = jnp.maximum(jnp.maximum(tops[0], tops[1]), jnp.maximum(tops[2], tops[3]))
    gains = {s: jnp.exp2(tops[s] - best) for s in order}
    inverse = 1.0 / sum(sums[s] * gains[s] for s in order)
    delta = sum(dots[s] * gains[s] for s in order) * inverse

    partcopies = [None]
    for s in range(1, parts):
        where = (dp, (me - s + parts) % parts)
        partcopies.append(remote(part.at[s], landed.at[s], part_send.at[s], part_recv.at[s], where))
    own_pair = None
    for s in (2, 1, 3, 0):
        prob = probs[s] * (gains[s] * inverse)
        dscore = (prob * (dprobs[s] - delta)).astype(jnp.bfloat16)
        dscores[s * rows:(s + 1) * rows, :] = dscore
        dkey = nn(dscore, qs[...])
        dvalue = nn(prob.astype(jnp.bfloat16), gs[...])
        if s:
            part[s, :, :width] = dkey.astype(jnp.bfloat16)
            part[s, :, width:] = dvalue.astype(jnp.bfloat16)
            partcopies[s].start()
        else:
            own_pair = (dkey, dvalue)
    sent += partcopies[1:]

    keys = kbuf[...].reshape(parts * rows, width)
    dquery = nn(keys.T, dscores[...]) * scale
    for h in range(heads):
        dq_ref[:, h * width:(h + 1) * width] = (
            dquery[:, h * rows:(h + 1) * rows].T.astype(jnp.bfloat16)
        )

    dkey, dvalue = own_pair
    for s in (1, 3, 2):
        partcopies[s].wait_recv()
        dkey = dkey + landed[s, :, :width].astype(jnp.float32)
        dvalue = dvalue + landed[s, :, width:].astype(jnp.float32)
    pair[0:rows, :width] = (dkey * scale).astype(jnp.bfloat16)
    pair[0:rows, width:] = dvalue.astype(jnp.bfloat16)
    paircopies = [None]
    for n in range(1, 6):
        copy = remote(
            pair.at[pl.ds(0, rows), :], pair.at[pl.ds(n * rows, rows), :],
            pair_send.at[n], pair_recv.at[n], close[n - 1],
        )
        paircopies.append(copy)
    for n in (3, 5, 2, 4, 1):
        paircopies[n].start()
    sent += paircopies[1:]

    for copy in owned:
        copy.wait()
    for copy in xcopies:
        copy.wait_recv()
    paircopies[1].wait_recv()
    last = parts - 1
    ends = (me == 0) | (me == last)
    beside = jnp.where(me == 0, 1, 2)
    first_turned = pair[0:2 * rows, :].T
    columns = [slice(z * chunk, (z + 1) * chunk) for z in range(2)]
    for a in range(2):
        for t in range(2):
            for z in range(2):
                early[a, t, z] = nn(first_turned, xab[a, t, 0:2 * rows, columns[z]])
    kept = (y, x)
    away = (place(1 - y, x, c), place(y, 1 - x, c))
    goals = [
        jnp.where((me == 0) | (me == 2), 3, 0),
        jnp.where(me % 2 == 0, 1, 2),
        jnp.where(ends, jnp.where(me == 0, 2, 1), jnp.where(me == 1, 3, 0)),
        me,
    ]
    halves = [pl.ds(h * width, width) for h in range(2)]

    @pl.when(ends)
    def _():
        zland[jnp.where(me == 0, 1, 3)] = jnp.zeros(zland.shape[1:], zland.dtype)

    for n in (2, 3, 4, 5):
        paircopies[n].wait_recv()
    for a in range(2):
        turned[a] = pair[(2 + 2 * a) * rows:(4 + 2 * a) * rows, :].T
    crosscopies = []
    for k, goal in enumerate(goals):
        a, z = goal // 2, goal % 2
        other = 1 - jnp.where(a == 0, y, x)
        late = xab[a, other, pl.ds(2 * rows, 2 * rows), pl.ds(pl.multiple_of(z * chunk, chunk), chunk)]
        cross[k] = (early[a, other, z] + nn(turned[a], late)).astype(jnp.bfloat16)
        where = (jnp.where(a == 0, away[0], away[1]), me)
        for h in range(2):
            copy = remote(
                cross.at[k, halves[h], :], crossed.at[k, halves[h], :],
                cross_send.at[k, h], cross_recv.at[k, h], where,
            )
            copy.start()
            crosscopies.append(copy)
    for a in range(2):
        for z in range(2):
            late = xab[a, kept[a], 2 * rows:4 * rows, columns[z]]
            zsum[2 * a + z] = early[a, kept[a], z] + nn(turned[a], late)
    sent += crosscopies

    for k, goal in enumerate(goals):
        device, to = goal, (goal - me + parts) % parts
        if k == 0:
            device, to = jnp.where(ends, beside, device), jnp.where(ends, 0, to)
        for h in range(2):
            crosscopies[2 * k + h].wait_recv()
            zsum[goal, halves[h], :] += crossed[k, halves[h], :].astype(jnp.float32)
            if k == 2:
                @pl.when(jnp.logical_not(ends))
                def _():
                    remote(
                        zout.at[0, halves[h], :], zland.at[0, halves[h], :],
                        z_send.at[0, h], z_recv.at[0, h], (dp, beside),
                    ).wait_recv()
                    zsum[goal, halves[h], :] += zland[0, halves[h], :].astype(jnp.float32)
            if k < 3:
                zout[k, halves[h], :] = zsum[goal, halves[h], :].astype(jnp.bfloat16)
                copy = remote(
                    zout.at[k, halves[h], :], zland.at[to, halves[h], :],
                    z_send.at[k, h], z_recv.at[to, h], (dp, device),
                )
                copy.start()
                sent.append(copy)

    def sum_in(n):
        for h in range(2):
            remote(
                zout.at[0, halves[h], :], zland.at[n, halves[h], :],
                z_send.at[0, h], z_recv.at[n, h], (dp, (me + n) % parts),
            ).wait_recv()

    pl.when(me != 0)(lambda: sum_in(1))
    pl.when(me != last)(lambda: sum_in(3))
    sum_in(2)
    final = zsum[me]
    for s in (1, 3, 2):
        final = final + zland[s].astype(jnp.float32)
    dw_ref[...] = (final * grad_scale).T.astype(jnp.bfloat16)
    for copy in sent:
        copy.wait_send()


def fused(layer_input, query_rows, key_rows, value_rows, grad_out, doc_lengths, block_order):
    rows, width = key_rows.shape[1:]
    model = layer_input.shape[2]
    heads = query_rows.shape[2] // width
    count, parts = lax.axis_size("dp"), lax.axis_size("ctx")
    chunk = model // (count * parts)
    lanes = rows * heads
    grad_scale = (count * rows * parts) ** (-0.5)
    low, full = jnp.bfloat16, jnp.float32
    vmem = pl.BlockSpec(memory_space=pltpu.VMEM)
    dma = pltpu.SemaphoreType.DMA

    def body(*refs):
        kernel(grad_scale, *refs)

    query_grad, weight_grad = pl.pallas_call(
        body,
        out_shape=(
            jax.ShapeDtypeStruct((rows, heads * width), low),
            jax.ShapeDtypeStruct((chunk, 2 * width), low),
        ),
        in_specs=[pl.BlockSpec(memory_space=pltpu.HBM)] * 7,
        out_specs=(vmem, vmem),
        scratch_shapes=[
            pltpu.SMEM(doc_lengths.shape, jnp.int32),
            pltpu.SMEM(block_order.shape, jnp.int32),
            dma((4 + 2 * heads,)),
            pltpu.VMEM((lanes, width), low),
            pltpu.VMEM((lanes, width), low),
            pltpu.VMEM((parts, rows, width), low),
            pltpu.VMEM((parts, rows, width), low),
            pltpu.VMEM((parts, rows, lanes), full),
            pltpu.VMEM((parts, rows, lanes), full),
            pltpu.VMEM((parts * rows, lanes), low),
            pltpu.VMEM((parts, rows, 2 * width), low),
            pltpu.VMEM((parts, rows, 2 * width), low),
            pltpu.VMEM((6 * rows, 2 * width), low),
            pltpu.VMEM((2, 2, 4 * rows, 2 * chunk), low),
            pltpu.VMEM((2, 2 * width, 2 * rows), low),
            pltpu.VMEM((2, 2, 2, 2 * width, chunk), full),
            pltpu.VMEM((4, 2 * width, chunk), low),
            pltpu.VMEM((4, 2 * width, chunk), low),
            pltpu.VMEM((4, 2 * width, chunk), full),
            pltpu.VMEM((4, 2 * width, chunk), low),
            pltpu.VMEM((4, 2 * width, chunk), low),
            dma((4,)), dma((4,)), dma((4,)), dma((4,)),
            dma((2, 8)), dma((2, 8)), dma((4,)),
            dma((4,)), dma((4,)), dma((6,)), dma((6,)),
            dma((4, 2)), dma((4, 2)), dma((4, 2)), dma((4, 2)),
        ],
        compiler_params=pltpu.CompilerParams(
            collective_id=0, has_side_effects=True, vmem_limit_bytes=60 * 1024 * 1024
        ),
    )(layer_input[0], query_rows[0], key_rows[0], value_rows[0], grad_out[0], doc_lengths, block_order)
    return (query_grad[None], weight_grad)


def solution(mesh):
    placed = (
        P("dp", "ctx", None),
        P("dp", "ctx", None),
        P("dp", "ctx", None),
        P("dp", "ctx", None),
        P("dp", "ctx", None),
        P("dp", None),
        P(),
    )
    return jax.shard_map(
        fused if dict(mesh.shape) == {"dp": 8, "ctx": 4} else by_rings,
        mesh=mesh,
        in_specs=placed,
        out_specs=(P("dp", "ctx", None), P(("dp", "ctx"), None)),
        check_vma=False,
    )
```
